32 devices in a mesh: batch: 4 (over x, core), head: 8 (over z, y).
Axes of the slice: x: 2, y: 2, z: 4, core: 2. Of those that a mesh axis runs over, the one named last changes fastest.
Arguments:
- token_ids: int32 [4, 2048], P('batch'), may hold values from 0 to 50303
- next_target: int32 [4, 2048], P('batch'), may hold values from 0 to 50303
- second_target: int32 [4, 2048], P('batch'), may hold values from 0 to 50303
- live_mask: int32 [4, 2048], P('batch'), may hold values 0 or 1
- row_lengths: int32 [4], P('batch'), may hold values from 1024 to 2048, as said below
- tables: float32 [3, 50304, 1024], P(None, 'head', 'batch'), may hold values from -0.65625 to 0.65625
- factor_head: float32 [1024, 160], P('batch', 'head'), may hold values from -0.375 to 0.375
- factor_shared: float32 [1024, 640], P('batch'), may hold values from -0.1875 to 0.1875
- project_out: float32 [1024, 1024], P('head', 'batch'), may hold values from -0.75 to 0.75
- feed_in: float32 [2, 1024, 2816], P(None, 'batch', 'head'), may hold values from -0.1875 to 0.1875
- feed_out: float32 [2816, 1024], P('head', 'batch'), may hold values from -0.109375 to 0.109375
- norm_gains: float32 [3, 1024], P(None, 'batch'), may hold values from 0.5 to 1.5
- tables_first: float32 [3, 50304, 1024], P(None, 'head', 'batch'), may hold values from -9.536743e-07 to 9.536743e-07
- factor_head_first: float32 [1024, 160], P('batch', 'head'), may hold values from -9.536743e-07 to 9.536743e-07
- factor_shared_first: float32 [1024, 640], P('batch'), may hold values from -9.536743e-07 to 9.536743e-07
- project_out_first: float32 [1024, 1024], P('head', 'batch'), may hold values from -9.536743e-07 to 9.536743e-07
- feed_in_first: float32 [2, 1024, 2816], P(None, 'batch', 'head'), may hold values from -9.536743e-07 to 9.536743e-07
- feed_out_first: float32 [2816, 1024], P('head', 'batch'), may hold values from -9.536743e-07 to 9.536743e-07
- norm_gains_first: float32 [3, 1024], P(None, 'batch'), may hold values from -3.8146973e-06 to 3.8146973e-06
- tables_second: float32 [3, 50304, 1024], P(None, 'head', 'batch'), may hold values from 7.270282e-14 to 9.69371e-13
- factor_head_second: float32 [1024, 160], P('batch', 'head'), may hold values from 7.270282e-14 to 9.69371e-13
- factor_shared_second: float32 [1024, 640], P('batch'), may hold values from 7.270282e-14 to 9.69371e-13
- project_out_second: float32 [1024, 1024], P('head', 'batch'), may hold values from 7.270282e-14 to 9.69371e-13
- feed_in_second: float32 [2, 1024, 2816], P(None, 'batch', 'head'), may hold values from 7.270282e-14 to 9.69371e-13
- feed_out_second: float32 [2816, 1024], P('head', 'batch'), may hold values from 7.270282e-14 to 9.69371e-13
- norm_gains_second: float32 [3, 1024], P(None, 'batch'), may hold values from 1.1632452e-12 to 1.5509935e-11
Outputs:
- loss: float32 [], replicated
- grad_norm: float32 [], replicated
- new_tables: float32 [3, 50304, 1024], P(None, 'head', 'batch')
- new_tables_first: float32 [3, 50304, 1024], P(None, 'head', 'batch')
- new_tables_second: float32 [3, 50304, 1024], P(None, 'head', 'batch')
- new_factor_head: float32 [1024, 160], P('batch', 'head')
- new_factor_head_first: float32 [1024, 160], P('batch', 'head')
- new_factor_head_second: float32 [1024, 160], P('batch', 'head')
- new_factor_shared: float32 [1024, 640], P('batch')
- new_factor_shared_first: float32 [1024, 640], P('batch')
- new_factor_shared_second: float32 [1024, 640], P('batch')
- new_project_out: float32 [1024, 1024], P('head', 'batch')
- new_project_out_first: float32 [1024, 1024], P('head', 'batch')
- new_project_out_second: float32 [1024, 1024], P('head', 'batch')
- new_feed_in: float32 [2, 1024, 2816], P(None, 'batch', 'head')
- new_feed_in_first: float32 [2, 1024, 2816], P(None, 'batch', 'head')
- new_feed_in_second: float32 [2, 1024, 2816], P(None, 'batch', 'head')
- new_feed_out: float32 [2816, 1024], P('head', 'batch')
- new_feed_out_first: float32 [2816, 1024], P('head', 'batch')
- new_feed_out_second: float32 [2816, 1024], P('head', 'batch')
- new_norm_gains: float32 [3, 1024], P(None, 'batch')
- new_norm_gains_first: float32 [3, 1024], P(None, 'batch')
- new_norm_gains_second: float32 [3, 1024], P(None, 'batch')
The draws below stay inside these ranges and needn't reach their ends.
Inputs may be any that keep to these rules, and one draw needn't show every extreme that they name: `row_lengths`: each row's length is 2048 or 1024, and each of the two occurs in every draw.
All inputs are finite; a program needn't handle non-finite values. No bound on the sum of `live_mask` on one device may be relied on, other than what follows from the above.
Results may differ from the reference program's by a relative error of at most 0.02.
The reference program's roundings to bfloat16 on the way count: a program that leaves them out, or rounds other values in their place, can miss the bound.
Values may be sent and summed in bfloat16 or wider, within the bound.
No kernel may reach another device: no remote copies, remote signals or barrier semaphores. Data moves between devices by JAX's collectives and lax.ppermute only.
A program may use at most 512 MiB of HBM per device.

```python
import math
import jax
import jax.numpy as jnp
import numpy as np
from jax import lax

D = 1024
H = 16
DH = 64
RQ = 6
RK = 2
FF = 2816
V = 50304
SEQ = 2048
STEP = 10
ROWS = 4


def draw_row_lengths(key, part):
    choose_full = jax.random.randint(jax.random.fold_in(key, 11), (ROWS,), 0, 2)
    full_at = jax.random.randint(jax.random.fold_in(key, 12), (), 0, ROWS)
    shift_by = jax.random.randint(jax.random.fold_in(key, 13), (), 1, ROWS)
    half_at = (full_at + shift_by) % ROWS
    places = jnp.arange(ROWS)
    choose_full = jnp.where(places == full_at, 1, choose_full)
    choose_full = jnp.where(places == half_at, 0, choose_full)
    return jnp.where(choose_full == 1, SEQ, SEQ // 2).astype(jnp.int32)


def draw_tables(key, part):
    entry_key = jax.random.fold_in(key, 21)
    scale_key = jax.random.fold_in(key, 22)
    entries = jnp.clip(jax.random.normal(entry_key, (3, V, D), jnp.float32), -6.0, 6.0)
    log_scale = jax.random.uniform(scale_key, (3, V, 1), jnp.float32, math.log(1.5), math.log(3.5))
    head_scale = jnp.exp(log_scale) * float(D) ** (-0.5)
    embed_scale = float(D // 4) ** (-0.5)
    slab_index = jnp.arange(3)[:, None, None]
    row_scale = jnp.where(slab_index == 0, embed_scale, head_scale)
    return (entries * row_scale).astype(jnp.float32)


def plant(drawn, stream_key, low, high):
    longest = drawn.shape.index(max(drawn.shape))
    spots = []
    for shift in (0, 1):
        where = [jax.random.randint(jax.random.fold_in(stream_key, axis), (), 0, length) for axis, length in enumerate(drawn.shape)]
        where[longest] = (where[longest] + shift) % drawn.shape[longest]
        spots.append(tuple(where))
    return drawn.at[spots[0]].set(low).at[spots[1]].set(high)


def block_levels(key, shape, shards, low, largest):
    factor_of, own = 1.0, jax.random.fold_in(key, 6)
    for dim, shards_of in shards:
        heights = jnp.exp(jax.random.uniform(jax.random.fold_in(own, dim), (shards_of,), jnp.float32, low / len(shards), largest / len(shards)))
        factor_of = factor_of * jnp.repeat(heights, shape[dim] // shards_of).reshape([-1 if axis == dim else 1 for axis in range(len(shape))])
    return factor_of


def cumulative_ranks(amount, slope):
    weights = [(1 << 20) // math.isqrt(rank ** slope) + 1 for rank in range(1, amount + 1)]
    scale = 1 + sum(weights) // (1 << 30)
    return np.cumsum(np.array([max(1, weight // scale) for weight in weights]))


def skewed_ids(key, dims, number_of, skew):
    grid = cumulative_ranks(number_of, skew)
    lot = jax.random.randint(jax.random.fold_in(key, 1), dims, 0, int(grid[number_of - 1]))
    standing = jnp.searchsorted(jnp.asarray(grid, jnp.int32), lot, side="right")
    return jax.random.permutation(jax.random.fold_in(key, 2), number_of)[standing].astype(jnp.int32)


def centred(rng, extent, scale, reach, pieces=(), held_as=jnp.bfloat16):
    gain = block_levels(rng, extent, pieces, -0.22, 0.18) if pieces else 1.0
    values = jax.random.normal(rng, extent, jnp.float32) * scale * gain
    return jnp.minimum(jnp.maximum(values, -reach), reach).astype(held_as)


def setup_inputs(seed: int = 0) -> dict:
    key_list = jax.random.split(jax.random.key(seed), 27)
    return {
        "token_ids": plant(skewed_ids(key_list[0], (ROWS, SEQ), V, 2), jax.random.fold_in(key_list[0], 3), 0, V - 1).astype(jnp.int32),
        "next_target": plant(skewed_ids(key_list[1], (ROWS, SEQ), V, 2), jax.random.fold_in(key_list[1], 3), 0, V - 1).astype(jnp.int32),
        "second_target": plant(skewed_ids(key_list[2], (ROWS, SEQ), V, 2), jax.random.fold_in(key_list[2], 3), 0, V - 1).astype(jnp.int32),
        "live_mask": plant((jax.random.randint(key_list[3], (ROWS, SEQ), 0, 4) < 3).astype(jnp.int32), jax.random.fold_in(key_list[3], 1), 0, 1),
        "row_lengths": draw_row_lengths(jax.random.fold_in(key_list[26], 71), 0),
        "tables": draw_tables(jax.random.fold_in(key_list[26], 71), 0),
        "factor_head": centred(key_list[6], (D, H * (RQ + 2 * RK)), (D // 4) ** -0.5, 0.375, ((0, 4), (1, 8)), jnp.float32),
        "factor_shared": centred(key_list[7], (D, (RQ + 2 * RK) * DH), D ** -0.5, 0.1875, ((0, 4),), jnp.float32),
        "project_out": centred(key_list[8], (H * DH, D), (H * DH // 16) ** -0.5, 0.75, ((0, 8), (1, 4)), jnp.float32),
        "feed_in": centred(key_list[9], (2, D, FF), D ** -0.5, 0.1875, ((1, 4), (2, 8)), jnp.float32),
        "feed_out": centred(key_list[10], (FF, D), FF ** -0.5, 0.109375, ((0, 8), (1, 4)), jnp.float32),
        "norm_gains": jnp.clip(1.0 + 0.1 * jax.random.normal(key_list[11], (3, D), jnp.float32), 0.5, 1.5),
        "tables_first": centred(key_list[12], (3, V, D), (0.11 * 0.02 * (3 * V * D + 10 * H * D + 10 * DH * D + H * DH * D + 3 * D * FF + 3 * D) ** -0.5), 9.5367431640625e-07, ((1, 8), (2, 4)), jnp.float32),
        "factor_head_first": centred(key_list[13], (D, H * (RQ + 2 * RK)), (0.11 * 0.02 * (3 * V * D + 10 * H * D + 10 * DH * D + H * DH * D + 3 * D * FF + 3 * D) ** -0.5), 9.5367431640625e-07, ((0, 4), (1, 8)), jnp.float32),
        "factor_shared_first": centred(key_list[14], (D, (RQ + 2 * RK) * DH), (0.11 * 0.02 * (3 * V * D + 10 * H * D + 10 * DH * D + H * DH * D + 3 * D * FF + 3 * D) ** -0.5), 9.5367431640625e-07, ((0, 4),), jnp.float32),
        "project_out_first": centred(key_list[15], (H * DH, D), (0.11 * 0.02 * (3 * V * D + 10 * H * D + 10 * DH * D + H * DH * D + 3 * D * FF + 3 * D) ** -0.5), 9.5367431640625e-07, ((0, 8), (1, 4)), jnp.float32),
        "feed_in_first": centred(key_list[16], (2, D, FF), (0.11 * 0.02 * (3 * V * D + 10 * H * D + 10 * DH * D + H * DH * D + 3 * D * FF + 3 * D) ** -0.5), 9.5367431640625e-07, ((1, 4), (2, 8)), jnp.float32),
        "feed_out_first": centred(key_list[17], (FF, D), (0.11 * 0.02 * (3 * V * D + 10 * H * D + 10 * DH * D + H * DH * D + 3 * D * FF + 3 * D) ** -0.5), 9.5367431640625e-07, ((0, 8), (1, 4)), jnp.float32),
        "norm_gains_first": centred(key_list[18], (3, D), (0.44 * 0.02 * (3 * V * D + 10 * H * D + 10 * DH * D + H * DH * D + 3 * D * FF + 3 * D) ** -0.5), 3.814697265625e-06, ((1, 4),), jnp.float32),
        "tables_second": jnp.clip(jnp.exp(math.log(9.6937095937083e-13) - 2.5902671 * jax.random.uniform(key_list[19], (3, V, D), jnp.float32) ** block_levels(key_list[19], (3, V, D), ((1, 8), (2, 4)), -0.2, 0.2)), 7.270282330806496e-14, 9.6937095937083e-13),
        "factor_head_second": jnp.clip(jnp.exp(math.log(9.6937095937083e-13) - 2.5902671 * jax.random.uniform(key_list[20], (D, H * (RQ + 2 * RK)), jnp.float32) ** block_levels(key_list[20], (D, H * (RQ + 2 * RK)), ((0, 4), (1, 8)), -0.2, 0.2)), 7.270282330806496e-14, 9.6937095937083e-13),
        "factor_shared_second": jnp.clip(jnp.exp(math.log(9.6937095937083e-13) - 2.5902671 * jax.random.uniform(key_list[21], (D, (RQ + 2 * RK) * DH), jnp.float32) ** block_levels(key_list[21], (D, (RQ + 2 * RK) * DH), ((0, 4),), -0.2, 0.2)), 7.270282330806496e-14, 9.6937095937083e-13),
        "project_out_second": jnp.clip(jnp.exp(math.log(9.6937095937083e-13) - 2.5902671 * jax.random.uniform(key_list[22], (H * DH, D), jnp.float32) ** block_levels(key_list[22], (H * DH, D), ((0, 8), (1, 4)), -0.2, 0.2)), 7.270282330806496e-14, 9.6937095937083e-13),
        "feed_in_second": jnp.clip(jnp.exp(math.log(9.6937095937083e-13) - 2.5902671 * jax.random.uniform(key_list[23], (2, D, FF), jnp.float32) ** block_levels(key_list[23], (2, D, FF), ((1, 4), (2, 8)), -0.2, 0.2)), 7.270282330806496e-14, 9.6937095937083e-13),
        "feed_out_second": jnp.clip(jnp.exp(math.log(9.6937095937083e-13) - 2.5902671 * jax.random.uniform(key_list[24], (FF, D), jnp.float32) ** block_levels(key_list[24], (FF, D), ((0, 8), (1, 4)), -0.2, 0.2)), 7.270282330806496e-14, 9.6937095937083e-13),
        "norm_gains_second": jnp.clip(jnp.exp(math.log(1.550993534993328e-11) - 2.5902671 * jax.random.uniform(key_list[25], (3, D), jnp.float32) ** block_levels(key_list[25], (3, D), ((1, 4),), -0.2, 0.2)), 1.1632451729290394e-12, 1.550993534993328e-11),
    }


HIGH = lax.Precision.HIGHEST
EPS = 1e-05
NEG = -1e+30
CLIP = 0.02
BETA_ONE = 0.9
BETA_TWO = 0.95
ADAM_EPS = 1e-08
RATES = (0.1, 0.1, 0.05, 0.2, 0.05, 0.03, 0.3)
DECAYS = (0.1, 0.1, 0.1, 0.1, 0.1, 0.1, 0.0)

@jax.custom_vjp
def low(v):
    return lax.optimization_barrier(v.astype(jnp.bfloat16)).astype(jnp.float32)

@jax.custom_vjp
def low_back(v):
    return v

def low_keep(v):
    return (low(v), None)

def low_pass(kept, grad):
    return (grad,)

def back_keep(v):
    return (v, None)

def back_low(kept, grad):
    return (low(grad),)
low.defvjp(low_keep, low_pass)
low_back.defvjp(back_keep, back_low)

def matmul(a, b):
    return jnp.dot(a, b, precision=HIGH, preferred_element_type=jnp.float32)

def rms_norm(values, gain_row):
    return values * lax.rsqrt(lax.optimization_barrier(jnp.mean(values * values, axis=-1, keepdims=True)) + EPS) * gain_row

def rope_tables(length, width):
    half_width = width // 2
    frequency = jnp.exp(-jnp.arange(half_width, dtype=jnp.float32) * (2.0 * math.log(10000.0) / width))
    angles = jnp.arange(length, dtype=jnp.float32)[:, None] * frequency[None, :]
    return (jnp.cos(angles), jnp.sin(angles))

def rotate(values, cosine_table, sine_table):
    half_width = values.shape[-1] // 2
    front_half = values[..., :half_width]
    back_half = values[..., half_width:]
    cos_b = cosine_table[:, None, :]
    sin_b = sine_table[:, None, :]
    return jnp.concatenate([front_half * cos_b - back_half * sin_b, back_half * cos_b + front_half * sin_b], axis=-1)

def factors(a_part, b_all, cosine_table, sine_table, head_count):
    a_part = a_part.reshape(a_part.shape[0], head_count, RQ + 2 * RK)
    b_all = b_all.reshape(b_all.shape[0], RQ + 2 * RK, DH)
    b_query = rotate(b_all[:, :RQ], cosine_table, sine_table)
    b_key = rotate(b_all[:, RQ:RQ + RK], cosine_table, sine_table)
    b_value = b_all[:, RQ + RK:]
    queries = jnp.einsum('nhr,nrd->nhd', a_part[:, :, :RQ], b_query, precision=HIGH) / RQ
    keys_all = jnp.einsum('nhr,nrd->nhd', a_part[:, :, RQ:RQ + RK], b_key, precision=HIGH) / RK
    values_all = jnp.einsum('nhr,nrd->nhd', a_part[:, :, RQ + RK:], b_value, precision=HIGH) / RK
    return (queries, keys_all, values_all)

def row_loss(weights, row_items, counts):
    tables, factor_head, factor_shared, project_out, feed_in, feed_out, norm_gains = weights
    tokens, next_row, second_row, live_next, live_second, length = row_items
    cosine_table, sine_table = rope_tables(SEQ, DH)
    stream_in = jnp.take(tables[0], tokens, axis=0)
    normed_one = low(rms_norm(stream_in, norm_gains[0]))
    a_all = low_back(matmul(normed_one, factor_head))
    b_all = low_back(matmul(normed_one, factor_shared))
    queries, keys_all, values_all = factors(a_all, b_all, cosine_table, sine_table, H)
    queries, keys_all, values_all = (low(queries), low(keys_all), low(values_all))
    scores = low_back(jnp.einsum('qhd,khd->hqk', queries, keys_all, precision=HIGH) * DH ** (-0.5))
    places = jnp.arange(SEQ)
    allowed = (places[None, :] <= places[:, None]) & (places[None, :] < length)
    scores = jnp.where(allowed[None], scores, NEG)
    weights_soft = low(jax.nn.softmax(scores, axis=-1))
    mixed_heads = jnp.einsum('hqk,khd->qhd', weights_soft, values_all, precision=HIGH)
    mixed_heads = low_back(low(mixed_heads)).reshape(SEQ, H * DH)
    stream_mid = stream_in + low_back(matmul(mixed_heads, project_out))
    normed_two = low(rms_norm(stream_mid, norm_gains[1]))
    gate_act = low_back(matmul(normed_two, feed_in[0]))
    up_act = low_back(matmul(normed_two, feed_in[1]))
    hidden = low(jax.nn.silu(gate_act) * up_act)
    stream_top = stream_mid + low_back(matmul(hidden, feed_out))
    final_norm = low(rms_norm(stream_top, norm_gains[2]))
    loss_sum = 0.0
    for j, target, live_row in ((1, next_row, live_next), (2, second_row, live_second)):
        logits = low_back(matmul(final_norm, tables[j].T))
        log_total = jax.nn.logsumexp(logits, axis=-1)
        picked = jnp.take_along_axis(logits, target[:, None], axis=-1)[:, 0]
        loss_sum = loss_sum + jnp.sum(live_row * (log_total - picked)) / counts[j - 1]
    return loss_sum

def total_loss(params, token_ids, next_target, second_target, live_next, live_second, row_lengths, counts):
    lowered = tuple((low(member) for member in params))
    checked = jax.checkpoint(row_loss)

    def accumulate(running, row_items):
        return (running + checked(lowered, row_items, counts), None)
    result, _ = lax.scan(accumulate, jnp.zeros((), jnp.float32), (token_ids, next_target, second_target, live_next, live_second, row_lengths))
    return result

def adam_update(weight, first, second, gradient, step_rate, decay_rate):
    first_new = BETA_ONE * first + (1.0 - BETA_ONE) * gradient
    second_new = BETA_TWO * second + (1.0 - BETA_TWO) * gradient * gradient
    first_hat = first_new / (1.0 - BETA_ONE ** STEP)
    second_hat = second_new / (1.0 - BETA_TWO ** STEP)
    weight_new = weight - step_rate * (first_hat / (jnp.sqrt(second_hat) + ADAM_EPS) + decay_rate * weight)
    return (weight_new, first_new, second_new)

def reference(token_ids, next_target, second_target, live_mask, row_lengths, tables, factor_head, factor_shared, project_out, feed_in, feed_out, norm_gains, tables_first, factor_head_first, factor_shared_first, project_out_first, feed_in_first, feed_out_first, norm_gains_first, tables_second, factor_head_second, factor_shared_second, project_out_second, feed_in_second, feed_out_second, norm_gains_second):
    places = jnp.arange(SEQ)
    live_float = live_mask.astype(jnp.float32)
    live_next = live_float * (places[None, :] < row_lengths[:, None] - 1).astype(jnp.float32)
    live_second = live_float * (places[None, :] < row_lengths[:, None] - 2).astype(jnp.float32)
    counts = jnp.stack([jnp.sum(live_next), jnp.sum(live_second)])
    params = (tables, factor_head, factor_shared, project_out, feed_in, feed_out, norm_gains)
    firsts = (tables_first, factor_head_first, factor_shared_first, project_out_first, feed_in_first, feed_out_first, norm_gains_first)
    seconds = (tables_second, factor_head_second, factor_shared_second, project_out_second, feed_in_second, feed_out_second, norm_gains_second)
    loss_value, pullback = jax.vjp(lambda *members: total_loss(members, token_ids, next_target, second_target, live_next, live_second, row_lengths, counts), *params)
    grads = pullback(jnp.ones_like(loss_value))
    squares = sum((jnp.sum(member * member) for member in grads))
    grad_norm = jnp.sqrt(squares)
    clip_scale = jnp.minimum(1.0, CLIP / grad_norm)
    updated = [adam_update(params[i], firsts[i], seconds[i], grads[i] * clip_scale, RATES[i], DECAYS[i]) for i in range(7)]
    return (loss_value, grad_norm, updated[0][0], updated[0][1], updated[0][2], updated[1][0], updated[1][1], updated[1][2], updated[2][0], updated[2][1], updated[2][2], updated[3][0], updated[3][1], updated[3][2], updated[4][0], updated[4][1], updated[4][2], updated[5][0], updated[5][1], updated[5][2], updated[6][0], updated[6][1], updated[6][2])
```

```python
import functools
import math

import jax
import jax.numpy as jnp
from jax import lax
from jax.experimental import pallas as pl
from jax.experimental.pallas import tpu as pltpu
from jax.sharding import PartitionSpec as P

DH = 64
RQ = 6
RK = 2
RT = RQ + 2 * RK
STEP = 10
EPS = 1e-05
NEG = -1e30
CLIP = 0.02
BETA_ONE = 0.9
BETA_TWO = 0.95
ADAM_EPS = 1e-08
RATES = (0.1, 0.1, 0.05, 0.2, 0.05, 0.03, 0.3)
DECAYS = (0.1, 0.1, 0.1, 0.1, 0.1, 0.1, 0.0)
OWNED = (True, True, False, True, True, True, False)
BF = jnp.bfloat16
F32 = jnp.float32
ALL = ("batch", "head")


def dot(left, right, contract_left, contract_right):
    return lax.dot_general(
        left, right, (((contract_left,), (contract_right,)), ((), ())),
        preferred_element_type=F32,
    )


def gather_small(values, axis, count):
    return lax.all_to_all(
        jnp.broadcast_to(values[None], (count,) + values.shape), axis, 0, 0
    )


def core_swap(values, count):
    return lax.ppermute(values, "batch", [(i, i ^ 1) for i in range(count)])


def swap(values, axis, count, step):
    return lax.ppermute(values, axis, [(i, i ^ step) for i in range(count)])


def bits(count):
    return [1 << i for i in range(count.bit_length() - 1)]


def by_distance(values, index):
    count = values.shape[0]
    shape = values.shape[1:]
    for step in bits(count):
        folded = values.reshape((count // (2 * step), 2, step) + shape)
        flip = ((index // step) % 2) == 1
        values = jnp.where(flip, folded[:, ::-1], folded).reshape((count,) + shape)
    return values


def batch_pieces(values, count):
    pieces = {0: values}
    for step in reversed(bits(count)):
        for k in list(pieces):
            pieces[k | step] = swap(pieces[k], "batch", count, step)
    return [pieces[k] for k in range(count)]


def batch_total(pieces, count):
    for step in bits(count):
        pieces = {
            k: pieces[k].astype(F32) + swap(pieces[k | step], "batch", count, step).astype(F32)
            for k in range(0, count, 2 * step)
        }
        if 2 * step < count:
            pieces = {k: part.astype(BF) for k, part in pieces.items()}
    return pieces[0]


def head_split(count):
    along_z = min(4, count)
    return along_z, count // along_z


def head_near(values, count):
    along_z, along_y = head_split(count)
    pieces = {0: values}
    for k in range(1, along_z):
        pieces[k * along_y] = swap(values, "head", count, k * along_y)
    for step in bits(along_y):
        for k in list(pieces):
            pieces[k | step] = swap(pieces[k], "head", count, step)
    return [pieces[k] for k in range(count)]


def head_total(pieces, count):
    along_z, along_y = head_split(count)
    for step in reversed(bits(along_y)):
        pieces = {
            k: (pieces[k].astype(F32) + swap(pieces[k | step], "head", count, step).astype(F32)).astype(BF)
            for k in range(count)
            if k % along_y < step
        }
    total = pieces[0].astype(F32)
    for k in range(1, along_z):
        total = total + swap(pieces[k * along_y], "head", count, k * along_y).astype(F32)
    return total


TILE = 256
CHUNK = 512


def vocab_blocks(vocab_local):
    block = vocab_local
    for parts in range(1, vocab_local + 1):
        if vocab_local % parts == 0 and vocab_local // parts <= 2112 and vocab_local // parts % 8 == 0:
            block = vocab_local // parts
            break
    edges = list(range(0, max(block - CHUNK // 2, 1), CHUNK)) + [block]
    return block, [(lo, hi - lo) for lo, hi in zip(edges[:-1], edges[1:])]


def table_chunk(table_refs, low, size):
    return jnp.concatenate([ref[0, low : low + size, :] for ref in table_refs], axis=-1)


def logits_kernel(nb, block, chunks, *refs):
    table_refs = refs[:nb]
    hf_ref, target_ref, e_ref, stat_ref = refs[nb:]
    first = pl.program_id(1) * block

    def one_tile(n, carry):
        cols = pl.ds(pl.multiple_of(n * TILE, TILE), TILE)
        rows = hf_ref[cols, :]
        target = target_ref[0, :, cols] - first
        for c, (low, size) in enumerate(chunks):
            logits = dot(table_chunk(table_refs, low, size), rows, 1, 1)
            peak = jnp.max(logits, axis=0, keepdims=True)
            shifted = jnp.exp(logits - peak)
            place = lax.broadcasted_iota(jnp.int32, logits.shape, 0)
            pick = jnp.where(place == target - low, logits, 0.0)
            e_ref[0, low : low + size, cols] = shifted.astype(BF)
            stat_ref[0, 0, 3 * c : 3 * c + 1, cols] = peak
            stat_ref[0, 0, 3 * c + 1 : 3 * c + 2, cols] = jnp.sum(shifted, axis=0, keepdims=True)
            stat_ref[0, 0, 3 * c + 2 : 3 * c + 3, cols] = jnp.sum(pick, axis=0, keepdims=True)
        return carry

    lax.fori_loop(0, hf_ref.shape[0] // TILE, one_tile, 0)


def logit_grad(e_ref, scale_ref, target, weight, c, low, size, cols):
    place = lax.broadcasted_iota(jnp.int32, (size, target.shape[1]), 0)
    soft = e_ref[0, low : low + size, cols].astype(F32) * scale_ref[0, 0, c : c + 1, cols]
    return (soft - jnp.where(place == target - low, weight, 0.0)).astype(BF)


def hidden_grad_kernel(nb, block, chunks, last, *refs):
    table_refs = refs[:nb]
    e_ref, scale_ref, target_ref, weight_ref, out_ref, total_ref = refs[nb:]
    first = pl.program_id(1) * block
    step = pl.program_id(0) * pl.num_programs(1) + pl.program_id(1)

    @pl.when(step == 0)
    def _():
        total_ref[...] = jnp.zeros_like(total_ref)

    def one_tile(n, carry):
        cols = pl.ds(pl.multiple_of(n * TILE, TILE), TILE)
        target = target_ref[0, :, cols] - first
        weight = weight_ref[0, :, cols]
        part = total_ref[cols, :]
        for c, (low, size) in enumerate(chunks):
            grad = logit_grad(e_ref, scale_ref, target, weight, c, low, size, cols)
            part = part + dot(grad, table_chunk(table_refs, low, size), 0, 0)
        total_ref[cols, :] = part
        return carry

    lax.fori_loop(0, total_ref.shape[0] // TILE, one_tile, 0)

    @pl.when(step == last)
    def _():
        out_ref[...] = total_ref[...].astype(out_ref.dtype)


def table_grad_kernel(nb, block, chunks, e_ref, scale_ref, target_ref, weight_ref, hf_ref, *out_refs):
    first = pl.program_id(1) * block
    d_local = out_refs[0].shape[2]
    every = slice(None)
    for c, (low, size) in enumerate(chunks):
        grad = logit_grad(
            e_ref, scale_ref, target_ref[0] - first, weight_ref[0], c, low, size, every
        )
        total = dot(grad, hf_ref[...], 1, 0).astype(BF)
        for k, ref in enumerate(out_refs):
            ref[0, low : low + size, :] = total[:, k * d_local : (k + 1) * d_local]


def attention_parts(a_ref, b_ref, q_ref, place_key_ref, place_query_ref):
    coef = a_ref[0]
    keys = ((coef[0:1] * b_ref[0] + coef[1:2] * b_ref[1]) / RK).astype(BF)
    values = ((coef[2:3] * b_ref[2] + coef[3:4] * b_ref[3]) / RK).astype(BF)
    scores = dot(q_ref[0], keys, 0, 0)
    scores = jnp.where(place_key_ref[...] <= place_query_ref[...], scores, NEG)
    shifted = jnp.exp(scores - jnp.max(scores, axis=1, keepdims=True))
    soft = shifted * (1.0 / jnp.sum(shifted, axis=1, keepdims=True))
    return keys, values, soft


def attend_kernel(a_ref, b_ref, q_ref, place_key_ref, place_query_ref, out_ref):
    _, values, soft = attention_parts(a_ref, b_ref, q_ref, place_key_ref, place_query_ref)
    out_ref[0] = dot(values, soft.astype(BF), 1, 1).astype(BF)


def attend_back_kernel(
    a_ref, b_ref, q_ref, place_key_ref, place_query_ref, grad_ref, dq_ref, da_ref, db_ref
):
    keys, values, soft = attention_parts(a_ref, b_ref, q_ref, place_key_ref, place_query_ref)
    grad = grad_ref[0]
    dprob = dot(grad, values, 0, 0)
    delta = jnp.sum(soft * dprob, axis=1, keepdims=True)
    dscore = (soft * (dprob - delta)).astype(BF)
    dq_ref[0] = dot(keys, dscore, 1, 1) * DH ** (-0.5)
    dkey = dot(q_ref[0], dscore, 1, 0) * (1.0 / RK)
    dvalue = dot(grad, soft.astype(BF), 1, 0) * (1.0 / RK)
    coef = a_ref[0]

    @pl.when(pl.program_id(0) == 0)
    def _():
        db_ref[...] = jnp.zeros_like(db_ref)

    for r, upstream in enumerate((dkey, dkey, dvalue, dvalue)):
        da_ref[0, r : r + 1, :] = jnp.sum(upstream * b_ref[r], axis=0, keepdims=True)
        db_ref[r] += upstream * coef[r : r + 1]


def attention_calls(heads, seq_len, own):
    a_spec = pl.BlockSpec((1, 2 * RK, seq_len), lambda h: (h, 0, 0))
    b_spec = pl.BlockSpec((2 * RK, DH, seq_len), lambda h: (0, 0, 0))
    q_spec = pl.BlockSpec((1, DH, own), lambda h: (h, 0, 0))
    key_spec = pl.BlockSpec((1, seq_len), lambda h: (0, 0))
    query_spec = pl.BlockSpec((own, 1), lambda h: (0, 0))
    params = pltpu.CompilerParams(vmem_limit_bytes=48 << 20)
    specs = [a_spec, b_spec, q_spec, key_spec, query_spec]
    cost = pl.CostEstimate(
        flops=32 * heads * own * seq_len * DH, bytes_accessed=24 * DH * seq_len, transcendentals=0
    )

    def attend(*operands):
        return pl.pallas_call(
            attend_kernel,
            grid=(heads,),
            in_specs=specs,
            out_specs=q_spec,
            out_shape=jax.ShapeDtypeStruct((heads, DH, own), BF),
            compiler_params=params,
            cost_estimate=cost,
        )(*operands)

    def attend_back(*operands):
        return pl.pallas_call(
            attend_back_kernel,
            grid=(heads,),
            in_specs=specs + [q_spec],
            out_specs=[q_spec, a_spec, b_spec],
            out_shape=[
                jax.ShapeDtypeStruct((heads, DH, own), F32),
                jax.ShapeDtypeStruct((heads, 2 * RK, seq_len), F32),
                jax.ShapeDtypeStruct((2 * RK, DH, seq_len), F32),
            ],
            compiler_params=params,
            cost_estimate=cost,
        )(*operands)

    return attend, attend_back


def head_calls(nb, vocab_local, d_local, seq_len):
    block, chunks = vocab_blocks(vocab_local)
    blocks = vocab_local // block
    width = nb * d_local
    grid = (2, blocks)
    table_spec = pl.BlockSpec((1, block, d_local), lambda j, v: (j, v, 0))
    whole = pl.BlockSpec((seq_len, width), lambda j, v: (0, 0))
    line = pl.BlockSpec((1, 1, seq_len), lambda j, v: (j, 0, 0))
    e_spec = pl.BlockSpec((1, block, seq_len), lambda j, v: (j, v, 0))
    stats = 3 * len(chunks)
    stat_spec = pl.BlockSpec((1, 1, stats, seq_len), lambda j, v: (j, v, 0, 0))
    scale_spec = pl.BlockSpec((1, 1, len(chunks), seq_len), lambda j, v: (j, v, 0, 0))
    params = pltpu.CompilerParams(vmem_limit_bytes=56 << 20)
    flops = 4 * vocab_local * seq_len * width
    cost = pl.CostEstimate(flops=flops, bytes_accessed=8 * vocab_local * (width + seq_len), transcendentals=0)

    def logits(pieces, hf, target):
        return pl.pallas_call(
            functools.partial(logits_kernel, nb, block, chunks),
            grid=grid,
            in_specs=[table_spec] * nb + [whole, line],
            out_specs=[e_spec, stat_spec],
            out_shape=[
                jax.ShapeDtypeStruct((2, vocab_local, seq_len), BF),
                jax.ShapeDtypeStruct((2, blocks, stats, seq_len), F32),
            ],
            compiler_params=params,
            cost_estimate=cost,
        )(*pieces, hf, target)

    def hidden_grad(pieces, e, scale, target, weight):
        return pl.pallas_call(
            functools.partial(hidden_grad_kernel, nb, block, chunks, 2 * blocks - 1),
            grid=grid,
            in_specs=[table_spec] * nb + [e_spec, scale_spec, line, line],
            out_specs=whole,
            out_shape=jax.ShapeDtypeStruct((seq_len, width), BF),
            scratch_shapes=[pltpu.VMEM((seq_len, width), F32)],
            compiler_params=params,
            cost_estimate=cost,
        )(*pieces, e, scale, target, weight)

    def table_grad(e, scale, target, weight, hf):
        return pl.pallas_call(
            functools.partial(table_grad_kernel, nb, block, chunks),
            grid=grid,
            in_specs=[e_spec, scale_spec, line, line, whole],
            out_specs=[table_spec] * nb,
            out_shape=[jax.ShapeDtypeStruct((2, vocab_local, d_local), BF)] * nb,
            compiler_params=params,
            cost_estimate=cost,
        )(e, scale, target, weight, hf)

    return logits, hidden_grad, table_grad


def total_all(values, counts):
    for axis, count in zip(ALL, counts):
        step = 1
        while step < count:
            values = values + lax.ppermute(
                values, axis, [(i, i ^ step) for i in range(count)]
            )
            step *= 2
    return values


def inv_rms(values):
    return lax.rsqrt(jnp.mean(values * values, axis=-1, keepdims=True) + EPS)


def norm_back(values, gain_row, upstream):
    inv_root = inv_rms(values)
    normed = values * inv_root
    gain_grad = jnp.sum(upstream * normed, axis=0)
    inner = upstream * gain_row
    grad_in = inv_root * (inner - normed * jnp.mean(inner * normed, axis=-1, keepdims=True))
    return (grad_in, gain_grad)


def device_order(row, heads):
    chunk = row.shape[-1] // (2 * heads)
    pieces = row.reshape(row.shape[:-1] + (2 * heads, chunk))
    front = pieces[..., :heads, :]
    back = pieces[..., heads:, :][..., ::-1, :]
    joined = jnp.concatenate([front, back], axis=-1)
    return joined


def turn(values, cosine, sine, sign):
    half = DH // 2
    front = values[..., :half, :]
    back = values[..., half:, :]
    if sign > 0:
        return jnp.concatenate([front * cosine - back * sine, back * cosine + front * sine], axis=-2)
    return jnp.concatenate([front * cosine + back * sine, back * cosine - front * sine], axis=-2)


def adam_update(weight, first, second, gradient, step_rate, decay_rate):
    first_new = BETA_ONE * first + (1.0 - BETA_ONE) * gradient
    second_new = BETA_TWO * second + (1.0 - BETA_TWO) * gradient * gradient
    first_hat = first_new / (1.0 - BETA_ONE**STEP)
    second_hat = second_new / (1.0 - BETA_TWO**STEP)
    weight_new = weight - step_rate * (
        first_hat / (jnp.sqrt(second_hat) + ADAM_EPS) + decay_rate * weight
    )
    return (weight_new, first_new, second_new)


def per_device(nb, nh, *args):
    (token_ids, next_target, second_target, live_mask, row_lengths) = args[:5]
    params, firsts, seconds = args[5:12], args[12:19], args[19:26]
    tables, factor_head, factor_shared, project_out, feed_in, feed_out, norm_gains = params
    head_index = lax.axis_index("head")
    core_index = lax.axis_index("batch") % 2
    vocab_local, d_local = tables.shape[1:]
    width = d_local * nb
    offset = head_index * vocab_local
    length = row_lengths[0]
    seq_len = token_ids.shape[1]
    own = seq_len // nh
    heads = factor_head.shape[1] * nh // RT
    ff_local = feed_out.shape[0]
    ff_half = ff_local // 2
    rows_out = project_out.shape[0]

    place_all = device_order(jnp.arange(seq_len), nh).reshape(seq_len)
    near = lambda rows: jnp.moveaxis(
        by_distance(jnp.moveaxis(rows.reshape(rows.shape[:-1] + (nh, own)), -2, 0), head_index), 0, -2
    ).reshape(rows.shape)
    place_own = lax.dynamic_slice_in_dim(place_all, head_index * own, own)
    ids_order = device_order(token_ids[0], nh)
    ids_all = gather_small(ids_order, "batch", nb)
    ids_own = lax.dynamic_index_in_dim(ids_order, head_index, 0, False)
    live_float = device_order(live_mask[0], nh).reshape(seq_len).astype(F32)
    live_both = jnp.stack(
        [
            live_float * (place_all < length - 1).astype(F32),
            live_float * (place_all < length - 2).astype(F32),
        ]
    )
    counts = jnp.sum(
        gather_small(jnp.sum(live_both, axis=1).reshape(1, 2), "batch", nb), axis=0
    ).reshape(2)
    token_weight = live_both / counts[:, None]

    batch_index = lax.axis_index("batch")
    gains = jnp.moveaxis(gather_small(norm_gains.astype(BF), "batch", nb), 0, 1).reshape(3, width).astype(F32)
    w_shared = gather_small(factor_shared.astype(BF), "batch", nb).reshape(width, RT * DH)
    w_head_part = gather_small(factor_head.astype(BF), "batch", nb).reshape(width, -1)
    w_head = gather_small(w_head_part.T, "head", nh).reshape(heads * RT, width)
    w_out_part = jnp.moveaxis(gather_small(project_out.astype(BF), "batch", nb), 0, 1).reshape(rows_out, width)
    feed_units = jnp.concatenate(
        [feed_in.astype(BF).transpose(0, 2, 1), feed_out.astype(BF)[None]], axis=0
    )
    feed_units = gather_small(feed_units, "batch", nb)
    feed_units = lax.dynamic_slice_in_dim(feed_units, core_index * ff_half, ff_half, 2)
    feed_units = jnp.moveaxis(feed_units, 0, 2).reshape(3 * ff_half, width)
    packed = lax.all_gather(jnp.concatenate([feed_units, w_out_part], axis=0), "head")
    feed_all = packed[:, : 3 * ff_half].reshape(nh, 3, ff_half, width)
    w_gate = feed_all[:, 0].reshape(nh * ff_half, width)
    w_up = feed_all[:, 1].reshape(nh * ff_half, width)
    w_down = feed_all[:, 2].reshape(nh * ff_half, width)
    w_out = packed[:, 3 * ff_half :].reshape(nh * rows_out, width)

    slots = max(16, 3 * own // 8 // 16 * 16)
    local_ids = ids_all - offset
    inside = (local_ids >= 0) & (local_ids < vocab_local)
    rank = jnp.cumsum(inside.astype(jnp.int32), axis=-1) - 1
    holder = jnp.arange(nh)[:, None]
    from_holder = (ids_own // vocab_local)[None, :] == holder
    rank_own = jnp.sum(
        jnp.where(from_holder, jnp.cumsum(from_holder.astype(jnp.int32), axis=1) - 1, 0), axis=0
    )
    most = jnp.max(
        jnp.sum(((ids_all // vocab_local)[:, :, None] == holder).astype(jnp.int32), axis=-1)
    )
    rounds = (most + slots - 1) // slots
    flat_tables = tables.reshape(3 * vocab_local, d_local)

    def round_ids(turn_index):
        wanted = turn_index * slots + jnp.arange(slots)
        match = (rank[:, :, None] == wanted[:, None]) & inside[:, :, None]
        found = jnp.sum(jnp.where(match, local_ids[:, :, None], 0), axis=-1)
        return jnp.where(jnp.any(match, axis=-1), found, vocab_local)

    def round_places(turn_index):
        wanted = (turn_index * slots + jnp.arange(slots))[None, None, :]
        match = from_holder.T[:, :, None] & (rank_own[:, None, None] == wanted)
        return match.astype(BF).reshape(own, nh * slots)

    def look_up(turn_index):
        picked = jnp.take(flat_tables, jnp.minimum(round_ids(turn_index).reshape(-1), vocab_local - 1), axis=0)
        shares = lax.all_to_all(picked.astype(BF).reshape(nb * nh, slots, d_local), ALL, 0, 0)
        shares = jnp.moveaxis(shares.reshape(nb, nh * slots, d_local), 0, 1).reshape(nh * slots, width)
        return dot(round_places(turn_index), shares, 1, 0)

    def give_back(turn_index, rows):
        sent = dot(round_places(turn_index), rows, 0, 0).astype(BF)
        sent = jnp.moveaxis(sent.reshape(nh, slots, nb, d_local), 2, 0).reshape(nb * nh, slots, d_local)
        shares = lax.all_to_all(sent, ALL, 0, 0).reshape(nb * nh * slots, d_local)
        return jax.ops.segment_sum(
            shares.astype(F32), round_ids(turn_index).reshape(-1), num_segments=vocab_local + 1
        )[:vocab_local]

    def all_rounds(one_round):
        return lax.fori_loop(1, rounds, lambda i, total: total + one_round(i), one_round(0))

    x0, head_tables = lax.optimization_barrier((all_rounds(look_up), tables[1:].astype(BF)))
    table_pieces = batch_pieces(head_tables, nb)

    h1 = (x0 * inv_rms(x0) * gains[0]).astype(BF)
    coef = dot(w_head, h1, 1, 1).reshape(heads, RT, own)
    shared = dot(w_shared, h1, 0, 1).reshape(RT, DH, own)
    frequency = jnp.exp(-jnp.arange(DH // 2, dtype=F32) * (2.0 * math.log(10000.0) / DH))
    angles = frequency[:, None] * place_own.astype(F32)[None, :]
    cosine, sine = jnp.cos(angles), jnp.sin(angles)
    b_query = turn(shared[:RQ], cosine, sine, 1)
    b_key = turn(shared[RQ : RQ + RK], cosine, sine, 1)
    b_value = shared[RQ + RK :]
    queries = sum(coef[:, r][:, None, :] * b_query[r][None] for r in range(RQ)) / RQ
    q_bf = (queries * DH ** (-0.5)).astype(BF)
    na = heads * 2 * RK
    kv_own = jnp.concatenate(
        [
            coef[:, RQ:].reshape(na, own),
            b_key.reshape(RK * DH, own),
            b_value.reshape(RK * DH, own),
        ],
        axis=0,
    )
    kv_all = jnp.concatenate(head_near(kv_own, nh), axis=1)
    a_all = kv_all[:na].reshape(heads, 2 * RK, seq_len)
    b_all = kv_all[na:].reshape(2 * RK, DH, seq_len)
    place_near = near(place_all)
    place_key = jnp.where(place_near < length, place_near, 2 * seq_len).reshape(1, seq_len)
    attend, attend_back = attention_calls(heads, seq_len, own)
    operands = (a_all, b_all, q_bf, place_key, place_own.reshape(own, 1))
    mixed = attend(*operands)
    mixed = mixed.reshape(heads * DH, own)
    x1 = x0 + dot(mixed, w_out, 0, 0)

    h2 = (x1 * inv_rms(x1) * gains[1]).astype(BF)
    h2_pair = jnp.concatenate([h2, core_swap(h2, nb)], axis=0)
    gate = dot(h2_pair, w_gate, 1, 1)
    up = dot(h2_pair, w_up, 1, 1)
    sig = jax.nn.sigmoid(gate)
    hidden = (gate * sig * up).astype(BF)
    down = dot(hidden, w_down, 1, 0)
    x2 = x1 + down[:own] + core_swap(down[own:], nb)

    hf = (x2 * inv_rms(x2) * gains[2]).astype(BF)
    hf = by_distance(hf.reshape(own, nb, d_local).swapaxes(0, 1), batch_index).swapaxes(0, 1).reshape(own, width)
    hf_all = jnp.concatenate(head_near(hf, nh), axis=0)

    call_logits, call_hidden, call_table = head_calls(nb, vocab_local, d_local, seq_len)
    targets = jnp.stack([device_order(next_target[0], nh), device_order(second_target[0], nh)])
    targets = near(targets.reshape(2, 1, seq_len)) - offset
    weight_near = near(token_weight)
    e_all, stats = call_logits(table_pieces, hf_all, targets)
    stats = stats.reshape(2, stats.shape[1], -1, 3, seq_len)
    peak_c = stats[:, :, :, 0]
    peak_l = jnp.max(peak_c, axis=(1, 2))
    total_l = jnp.sum(stats[:, :, :, 1] * jnp.exp(peak_c - peak_l[:, None, None]), axis=(1, 2))
    pick_l = jnp.sum(stats[:, :, :, 2], axis=(1, 2))
    found = gather_small(near(jnp.stack([peak_l, total_l, pick_l])), "head", nh)
    peak_g = jnp.max(found[:, 0], axis=0)
    total_g = jnp.sum(found[:, 1] * jnp.exp(found[:, 0] - peak_g), axis=0)
    lse = peak_g + jnp.log(total_g)
    loss_local = jnp.sum(token_weight * (lse - jnp.sum(found[:, 2], axis=0)))
    scale_c = jnp.exp(peak_c - near(lse)[:, None, None]) * weight_near[:, None, None]
    weight_line = weight_near.reshape(2, 1, seq_len)
    dhf_part = call_hidden(table_pieces, e_all, scale_c, targets, weight_line)
    dhf = head_total([dhf_part[k * own : (k + 1) * own] for k in range(nh)], nh)
    dhf = by_distance(dhf.reshape(own, nb, d_local).swapaxes(0, 1), batch_index).swapaxes(0, 1).reshape(own, width)
    dhf, table_grads = lax.optimization_barrier(
        (dhf, tuple(call_table(e_all, scale_c, targets, weight_line, hf_all)))
    )
    head_red = batch_total(table_grads, nb)

    dx2, gain_top = norm_back(x2, gains[2], dhf)
    e_own = dx2.astype(BF)
    e_pair = jnp.concatenate([e_own, core_swap(e_own, nb)], axis=0)
    dhidden = dot(e_pair, w_down, 1, 1)
    dgate = (dhidden * up * sig * (1.0 + gate * (1.0 - sig))).astype(BF)
    dup = (dhidden * gate * sig).astype(BF)
    g_gate = dot(dgate, h2_pair, 0, 0)
    g_up = dot(dup, h2_pair, 0, 0)
    g_down = dot(hidden, e_pair, 0, 0)
    dh2_pair = dot(dgate, w_gate, 1, 0) + dot(dup, w_up, 1, 0)
    dh2 = dh2_pair[:own] + core_swap(dh2_pair[own:], nb)
    back2, gain_two = norm_back(x1, gains[1], dh2)
    dx1 = dx2 + back2

    c_own = dx1.astype(BF)
    g_out = dot(mixed, c_own, 1, 0)
    g_feed = jnp.stack([g_gate, g_up, g_down]).astype(BF).reshape(3, nh, ff_half, width)
    g_pack = jnp.concatenate(
        [
            jnp.moveaxis(g_feed, 0, 1).reshape(nh, 3 * ff_half, width),
            g_out.astype(BF).reshape(nh, rows_out, width),
        ],
        axis=1,
    )
    g_pack = lax.psum_scatter(g_pack, "head", scatter_dimension=0)
    g_pack = lax.all_to_all(
        jnp.moveaxis(g_pack.reshape(3 * ff_half + rows_out, nb, d_local), 1, 0), "batch", 0, 0
    ).astype(F32)
    red_feed = jnp.sum(
        g_pack[:, : 3 * ff_half].reshape(nb // 2, 2, 3, ff_half, d_local), axis=0
    )
    red_feed = jnp.moveaxis(red_feed, 0, 1).reshape(3, ff_local, d_local)
    feed_in_red = red_feed[:2].transpose(0, 2, 1)
    feed_out_red = red_feed[2]
    out_red = jnp.sum(g_pack[:, 3 * ff_half :], axis=0)

    dmixed = dot(w_out, c_own, 1, 1).astype(BF).reshape(heads, DH, own)
    dq, da_kv, db_kv = attend_back(*operands, dmixed)
    dkv = jnp.concatenate([da_kv.reshape(na, seq_len), db_kv.reshape(2 * RK * DH, seq_len)], axis=0).astype(BF)
    dkv = head_total([dkv[:, k * own : (k + 1) * own] for k in range(nh)], nh)
    da_q = jnp.stack([jnp.sum(dq * b_query[r][None], axis=1) for r in range(RQ)], axis=1) / RQ
    db_q = jnp.stack([jnp.sum(dq * coef[:, r][:, None, :], axis=0) for r in range(RQ)]) / RQ
    dcoef = jnp.concatenate([da_q, dkv[:na].reshape(heads, 2 * RK, own)], axis=1)
    dcoef = dcoef.reshape(heads * RT, own).astype(BF)
    dshared = jnp.concatenate(
        [
            turn(db_q, cosine, sine, -1),
            turn(dkv[na : na + RK * DH].reshape(RK, DH, own), cosine, sine, -1),
            dkv[na + RK * DH :].reshape(RK, DH, own),
        ],
        axis=0,
    ).reshape(RT * DH, own).astype(BF)
    dh1 = dot(dcoef, w_head, 0, 0) + dot(dshared, w_shared, 0, 1)
    back1, gain_one = norm_back(x0, gains[0], dh1)
    dx0 = (dx1 + back1).astype(BF)

    g_coef = dot(h1, dcoef, 0, 1)
    g_shared = dot(h1, dshared, 0, 1)
    g_gain = jnp.stack([gain_one, gain_two, gain_top]).T
    g_small = jnp.concatenate([g_coef, g_shared, g_gain], axis=1).astype(BF)
    cols = g_small.shape[1]
    g_small = lax.all_to_all(g_small.reshape(nb, d_local, cols), "batch", 0, 0)
    g_small = jnp.sum(g_small.astype(F32), axis=0).astype(BF)
    g_small = lax.all_to_all(g_small.reshape(nh, d_local // nh, cols), "head", 0, 0)
    g_small = jnp.sum(g_small.astype(F32), axis=0).astype(BF)
    g_small = gather_small(g_small, "head", nh).reshape(d_local, cols).astype(F32)
    nc = heads * RT
    head_red_f = lax.dynamic_slice_in_dim(g_small[:, :nc], head_index * (nc // nh), nc // nh, 1)
    shared_red = g_small[:, nc : nc + RT * DH]
    gain_red = g_small[:, nc + RT * DH :].T

    embed_red = all_rounds(lambda turn_index: give_back(turn_index, dx0))

    grads = (None, head_red_f, shared_red, out_red, feed_in_red, feed_out_red, gain_red)
    owner_flag = (head_index == 0).astype(F32)
    squares = jnp.sum(embed_red * embed_red) + jnp.sum(head_red * head_red)
    for i in range(1, 7):
        part = jnp.sum(grads[i] * grads[i])
        squares = squares + (part if OWNED[i] else part * owner_flag)
    both = total_all(jnp.stack([squares, loss_local * owner_flag]).reshape(1, 2), (nb, nh))
    grad_norm = jnp.sqrt(both[0, 0])
    scale = jnp.minimum(1.0, CLIP / grad_norm)
    table_grad = jnp.concatenate([embed_red[None], head_red], axis=0)
    grads = (table_grad,) + grads[1:]
    outs = [both[0, 1], grad_norm]
    for i in range(7):
        outs.extend(
            adam_update(params[i], firsts[i], seconds[i], grads[i] * scale, RATES[i], DECAYS[i])
        )
    return tuple(outs)


def solution(mesh):
    nb, nh = mesh.shape["batch"], mesh.shape["head"]
    row = P("batch", None)
    weights = (
        P(None, "head", "batch"),
        P("batch", "head"),
        P("batch", None),
        P("head", "batch"),
        P(None, "batch", "head"),
        P("head", "batch"),
        P(None, "batch"),
    )
    return jax.shard_map(
        lambda *args: per_device(nb, nh, *args),
        mesh=mesh,
        in_specs=(row, row, row, row, P("batch")) + weights * 3,
        out_specs=(P(), P()) + tuple(spec for spec in weights for _ in range(3)),
        check_vma=False,
    )
```
